128 devices in a mesh: short: 16 (over z, y), long: 8 (over x, core).
Axes of the slice: x: 4, y: 4, z: 4, core: 2. Of those that a mesh axis runs over, the one named last changes fastest.
Arguments:
- query: bfloat16 [131072, 8, 128], P(('long', 'short')), may hold values from -6 to 6
- key: bfloat16 [131072, 8, 128], P(('long', 'short')), may hold values from -6 to 6
- value: bfloat16 [131072, 8, 128], P(('long', 'short')), may hold values from -6 to 6
- level_weight: float32 [8, 20, 131072], P(None, None, ('long', 'short')), may hold values from 0.25 to 1.75
Outputs:
- attended: bfloat16 [131072, 8, 128], P(('long', 'short'))
The draws below stay inside these ranges and needn't reach their ends.
All inputs are finite; a program needn't handle non-finite values.
Results may differ from the reference program's by a relative error of at most 0.0019.
Values sent between devices are 32-bit elements; how exact they have to be, the bound alone decides.
No kernel may reach another device: no remote copies, remote signals or barrier semaphores. Data moves between devices by JAX's collectives and lax.ppermute only.
A program may use at most 128 MiB of HBM per device.

```python
import jax
import jax.numpy as jnp
from jax import lax

H = 8
DH = 128
TOK_DEV = 1024
LEVELS = 20
TOKENS = 131072
N_SHORT = 16
N_LONG = 8


def block_scale(stream_key, extent, cuts, smallest, largest):
    def one(axis_at, parts):
        draws = jax.random.uniform(jax.random.fold_in(jax.random.fold_in(stream_key, 6), axis_at), (parts,), jnp.float32, smallest / len(cuts), largest / len(cuts))
        return jnp.repeat(jnp.exp(draws), extent[axis_at] // parts).reshape((-1,) + (1,) * (len(extent) - axis_at - 1))

    level = one(*cuts[0])
    for cut in cuts[1:]:
        level = level * one(*cut)
    return level


def centred(stream_key, dims, deviation, limit, pieces=(), held_as=jnp.bfloat16):
    result = jax.random.normal(stream_key, dims, jnp.float32) * deviation
    if len(pieces) > 0:
        result = block_scale(stream_key, dims, pieces, -0.22, 0.18) * result
    return jnp.clip(result, min=-limit, max=limit).astype(held_as)


def setup_inputs(seed: int = 0) -> dict:
    streams_of = jax.random.split(jax.random.key(seed), 5)
    return {
        "query": centred(streams_of[0], (TOKENS, H, DH), 1.0, 6.0, ((0, 128),)),
        "key": centred(streams_of[1], (TOKENS, H, DH), 1.0, 6.0, ((0, 128),)),
        "value": centred(streams_of[2], (TOKENS, H, DH), 1.0, 6.0, ((0, 128),)),
        "level_weight": jnp.clip(0.25 + 1.5 * jax.random.uniform(streams_of[3], (H, LEVELS, TOKENS), jnp.float32) ** block_scale(streams_of[3], (H, LEVELS, TOKENS), ((2, 128),), -0.2, 0.2), 0.25, 1.75),
    }


EPSILON = 1e-06

def level_table(row_ids, col_ids, local_bits):
    differ = jnp.bitwise_xor(row_ids[:, None], col_ids[None, :])
    levels = jnp.zeros(differ.shape, jnp.int32)
    for bit_no in range(local_bits):
        levels = levels + (differ >= 1 << bit_no).astype(jnp.int32)
    return levels

def near_part(query_blk, key_blk, value_blk, weight_blk):
    length = query_blk.shape[0]
    local_bits = length.bit_length() - 1
    block_rows = min(512, length)
    col_ids = jnp.arange(length, dtype=jnp.int32)
    key_full = key_blk.astype(jnp.float32)
    value_full = value_blk.astype(jnp.float32)
    outputs = []
    for row_start in range(0, length, block_rows):
        row_ids = row_start + jnp.arange(block_rows, dtype=jnp.int32)
        levels = level_table(row_ids, col_ids, local_bits)
        causal = col_ids[None, :] <= row_ids[:, None]
        scores = jnp.einsum('thd,shd->hts', query_blk[row_start:row_start + block_rows].astype(jnp.float32), key_full)
        mixing = jnp.zeros(scores.shape, jnp.float32)
        for level_no in range(local_bits + 1):
            chosen = jnp.where(levels == level_no, 1.0, 0.0).astype(jnp.float32)
            mixing = mixing + chosen[None] * weight_blk[:, level_no, row_start:row_start + block_rows][:, :, None]
        weighted = jnp.where(causal[None], mixing * scores, 0.0).astype(jnp.bfloat16)
        outputs.append(jnp.einsum('hts,she->the', weighted.astype(jnp.float32), value_full))
    return jnp.concatenate(outputs, 0)

def far_part(query_blk, bucket_blk, weight_blk, local_bits):
    bit_count = bucket_blk.shape[0]
    products = jnp.einsum('thd,bhde->bthe', query_blk.astype(jnp.float32), bucket_blk, precision=lax.Precision.HIGHEST)
    gains = jnp.transpose(weight_blk[:, local_bits + 1:local_bits + 1 + bit_count, :], (1, 2, 0))
    return lax.optimization_barrier(jnp.sum(products * gains[..., None], 0))

def finish(total):
    scale = lax.rsqrt(lax.optimization_barrier(jnp.mean(total * total, -1, keepdims=True)) + EPSILON)
    return (total * scale).astype(jnp.bfloat16)

def state_of(inputs):
    return jnp.einsum('thd,the->hde', inputs[0].astype(jnp.float32), inputs[1].astype(jnp.float32))

def reference(query, key, value, level_weight):
    blocks = N_SHORT * N_LONG
    block_bits = blocks.bit_length() - 1
    local_bits = TOK_DEV.bit_length() - 1
    heads = query.shape[1]
    width = query.shape[2]
    query_b = query.reshape(blocks, TOK_DEV, heads, width)
    key_b = key.reshape(blocks, TOK_DEV, heads, width)
    value_b = value.reshape(blocks, TOK_DEV, heads, width)
    weight_b = jnp.transpose(level_weight.reshape(heads, LEVELS, blocks, TOK_DEV), (2, 0, 1, 3))
    states = lax.map(state_of, (key_b, value_b))
    block_ids = jnp.arange(blocks, dtype=jnp.int32)
    level_sum = states
    buckets = []
    for bit_no in range(block_bits):
        partner = jnp.bitwise_xor(block_ids >> bit_no, 1).astype(jnp.int32)
        chosen = jnp.take(level_sum, partner, axis=0)
        is_set = block_ids >> bit_no & 1 == 1
        buckets.append(jnp.where(is_set[:, None, None, None], chosen, 0.0))
        level_sum = level_sum.reshape((-1, 2) + level_sum.shape[1:]).sum(1)
    bucket_all = jnp.stack(buckets, 1)

    def one_block(items):
        query_blk, key_blk, value_blk, weight_blk, bucket_blk = items
        total = near_part(query_blk, key_blk, value_blk, weight_blk) + far_part(query_blk, bucket_blk, weight_blk, local_bits)
        return finish(total)
    attended = lax.map(one_block, (query_b, key_b, value_b, weight_b, bucket_all))
    return attended.reshape(blocks * TOK_DEV, heads, width)
```

```python
import jax
import jax.numpy as jnp
from jax import lax
from jax.experimental import pallas as pl
from jax.experimental.pallas import tpu as pltpu
from jax.sharding import PartitionSpec as P

EPSILON = 1e-06
VMEM_LIMIT = 56 * 1024 * 1024
NT = (((1,), (1,)), ((), ()))
NN = (((1,), (0,)), ((), ()))


def dot(lhs, rhs, dims):
    return lax.dot_general(lhs, rhs, dims, preferred_element_type=jnp.float32)


def state_kernel(key_ref, value_ref, state_ref, key_out, value_out, key_f, value_f):
    @pl.when(pl.program_id(0) == 0)
    def _():
        state_ref[...] = jnp.zeros_like(state_ref)

    key_f[...] = key_ref[...].astype(jnp.float32)
    value_f[...] = value_ref[...].astype(jnp.float32)
    for head in range(key_ref.shape[1]):
        key_h = key_f[:, head, :].astype(jnp.bfloat16)
        value_t = value_f[:, head, :].T.astype(jnp.bfloat16)
        key_out[head] = key_h
        value_out[head] = value_t
        state_ref[head] += dot(value_t, key_h, NN)


def states(key, value, rows=256):
    length, heads, width = key.shape
    whole = pl.BlockSpec((rows, heads, width), lambda i: (i, 0, 0))
    return pl.pallas_call(
        state_kernel,
        grid=(length // rows,),
        in_specs=[whole, whole],
        out_specs=[
            pl.BlockSpec((heads, width, width), lambda i: (0, 0, 0)),
            pl.BlockSpec((heads, rows, width), lambda i: (0, i, 0)),
            pl.BlockSpec((heads, width, rows), lambda i: (0, 0, i)),
        ],
        out_shape=[
            jax.ShapeDtypeStruct((heads, width, width), jnp.float32),
            jax.ShapeDtypeStruct((heads, length, width), jnp.bfloat16),
            jax.ShapeDtypeStruct((heads, width, length), jnp.bfloat16),
        ],
        scratch_shapes=[pltpu.VMEM((rows, heads, width), jnp.float32)] * 2,
        compiler_params=pltpu.CompilerParams(vmem_limit_bytes=VMEM_LIMIT),
        cost_estimate=pl.CostEstimate(flops=10**9, bytes_accessed=8 * 2**20, transcendentals=0),
        name="states",
    )(key, value)


def query_kernel(query_ref, query_out, query_f):
    query_f[...] = query_ref[...].astype(jnp.float32)
    for head in range(query_ref.shape[1]):
        query_out[head] = query_f[:, head, :].astype(jnp.bfloat16)


def by_head(query, rows=256):
    length, heads, width = query.shape
    return pl.pallas_call(
        query_kernel,
        grid=(length // rows,),
        in_specs=[pl.BlockSpec((rows, heads, width), lambda i: (i, 0, 0))],
        out_specs=pl.BlockSpec((heads, rows, width), lambda i: (0, i, 0)),
        out_shape=jax.ShapeDtypeStruct((heads, length, width), jnp.bfloat16),
        scratch_shapes=[pltpu.VMEM((rows, heads, width), jnp.float32)],
        compiler_params=pltpu.CompilerParams(vmem_limit_bytes=VMEM_LIMIT),
        cost_estimate=pl.CostEstimate(flops=10**6, bytes_accessed=4 * 2**20, transcendentals=0),
        name="by_head",
    )(query)


TILE = 256


def near_kernel(query_ref, key_ref, value_ref, weight_ref, near_ref):
    length = query_ref.shape[1]
    head = pl.program_id(0)
    groups = TILE // 8
    group_r = lax.broadcasted_iota(jnp.int32, (groups, TILE), 0)
    group_t = lax.broadcasted_iota(jnp.int32, (groups, TILE), 1) >> 3
    apart = group_r ^ group_t
    later = group_t > group_r
    inner_s = lax.broadcasted_iota(jnp.int32, (8, TILE), 0)
    inner_t = lax.broadcasted_iota(jnp.int32, (8, TILE), 1) & 7
    inner = inner_s ^ inner_t
    same = (
        lax.broadcasted_iota(jnp.int32, (groups, 8, TILE), 0)
        == lax.broadcasted_iota(jnp.int32, (groups, 8, TILE), 2) >> 3
    )
    for tile in range(length // TILE):
        cols = slice(tile * TILE, (tile + 1) * TILE)

        def gain(level):
            return weight_ref[level, pl.ds(head, 1), cols]

        query = query_ref[0, cols, :]
        parts = []
        for other in range(tile):
            scores = dot(key_ref[0, other * TILE : (other + 1) * TILE, :], query, NT)
            parts.append((scores * gain(8 + (tile ^ other).bit_length())).astype(jnp.bfloat16))
        outer = gain(4)
        for level in range(5, 9):
            outer = jnp.where(apart >= 1 << (level - 4), gain(level), outer)
        outer = jnp.where(later, outer, 0.0)
        small = gain(0)
        for level in range(1, 4):
            small = jnp.where(inner >= 1 << (level - 1), gain(level), small)
        small = jnp.where(inner_s <= inner_t, small, 0.0)
        mixing = jnp.where(same, small[None], outer[:, None, :]).reshape(TILE, TILE)
        scores = dot(key_ref[0, cols, :], query, NT)
        parts.append((scores * mixing).astype(jnp.bfloat16))
        weighted = jnp.concatenate(parts, 0)
        near_ref[0, :, cols] = dot(value_ref[0, :, : (tile + 1) * TILE], weighted, NN)


def near_part(query, key, value, level_weight):
    heads, length, width = query.shape
    levels = level_weight.shape[0]
    rows = pl.BlockSpec((1, length, width), lambda h: (h, 0, 0))
    flat = pl.BlockSpec((1, width, length), lambda h: (h, 0, 0))
    return pl.pallas_call(
        near_kernel,
        grid=(heads,),
        in_specs=[rows, rows, flat, pl.BlockSpec((levels, heads, length), lambda h: (0, 0, 0))],
        out_specs=flat,
        out_shape=jax.ShapeDtypeStruct((heads, width, length), jnp.float32),
        compiler_params=pltpu.CompilerParams(vmem_limit_bytes=VMEM_LIMIT),
        cost_estimate=pl.CostEstimate(
            flops=8 * 10**9, bytes_accessed=12 * 2**20, transcendentals=0
        ),
        name="near",
    )(query, key, value, level_weight)


def far_kernel(local_bits, block_ref, query_ref, near_ref, weight_ref, *rest):
    *bucket_refs, out_ref, split, total_f = rest
    bits = len(bucket_refs)
    heads, rows, width = query_ref.shape

    @pl.when(pl.program_id(0) == 0)
    def _():
        for bit in range(bits):
            for head in range(heads):
                bucket = bucket_refs[bit][head]
                high = bucket.astype(jnp.bfloat16)
                low = (bucket - high.astype(jnp.float32)).astype(jnp.bfloat16)
                split[head, bit * width : (bit + 1) * width, :width] = high
                split[head, bit * width : (bit + 1) * width, width:] = low

    block = block_ref[0]
    for head in range(heads):
        query = query_ref[head]
        products = dot(split[head], jnp.concatenate([query, query], 1), NT)
        total = near_ref[head]
        for bit in range(bits):
            level = local_bits + 1 + bit
            gain = weight_ref[level, head : head + 1, :]
            gain = jnp.where((block >> bit) & 1 == 1, gain, 0.0)
            total = total + products[bit * width : (bit + 1) * width, :] * gain
        mean = jnp.sum(total * total, 0, keepdims=True) * (1.0 / width)
        total = total * lax.rsqrt(mean + EPSILON)
        total_f[:, head, :] = total.T
    out_ref[...] = total_f[...].astype(jnp.bfloat16)


def finish(block, query, near, level_weight, buckets, rows=256):
    heads, length, width = query.shape
    levels = level_weight.shape[0]
    local_bits = length.bit_length() - 1
    bits = len(buckets)
    return pl.pallas_call(
        lambda *refs: far_kernel(local_bits, *refs),
        grid=(length // rows,),
        in_specs=[
            pl.BlockSpec(memory_space=pltpu.SMEM),
            pl.BlockSpec((heads, rows, width), lambda i: (0, i, 0)),
            pl.BlockSpec((heads, width, rows), lambda i: (0, 0, i)),
            pl.BlockSpec((levels, heads, rows), lambda i: (0, 0, i)),
        ]
        + [pl.BlockSpec((heads, width, width), lambda i: (0, 0, 0))] * bits,
        out_specs=pl.BlockSpec((rows, heads, width), lambda i: (i, 0, 0)),
        out_shape=jax.ShapeDtypeStruct((length, heads, width), jnp.bfloat16),
        scratch_shapes=[
            pltpu.VMEM((heads, bits * width, 2 * width), jnp.bfloat16),
            pltpu.VMEM((rows, heads, width), jnp.float32),
        ],
        compiler_params=pltpu.CompilerParams(vmem_limit_bytes=VMEM_LIMIT),
        cost_estimate=pl.CostEstimate(
            flops=8 * 10**9, bytes_accessed=12 * 2**20, transcendentals=0
        ),
        name="finish",
    )(block, query, near, level_weight, *buckets)


def swap(value, axis, bit):
    size = lax.axis_size(axis)
    return lax.ppermute(value, axis, [(i, partner(i, axis, bit)) for i in range(size)])


def partner(i, axis, bit):
    crossing = (1, 3) if axis == "short" else (2,)
    return i ^ (1 << bit) ^ (1 << (bit - 1)) if bit in crossing else i ^ (1 << bit)


def tree(state):
    buckets = []
    group = state
    for axis in ("short", "long"):
        for bit in range(lax.axis_size(axis).bit_length() - 1):
            other = swap(group, axis, bit)
            buckets.append(other)
            group = group + other
    return buckets


def per_device(query, key, value, level_weight):
    level_weight = jnp.transpose(level_weight, (1, 0, 2))
    state, key_h, value_t = states(key, value)
    block = lax.axis_index("long") * lax.axis_size("short") + lax.axis_index("short")
    buckets = tree(state)
    query_h = by_head(query)
    near = near_part(query_h, key_h, value_t, level_weight)
    return finish(block.astype(jnp.int32)[None], query_h, near, level_weight, buckets)


def solution(mesh):
    return jax.shard_map(
        per_device,
        mesh=mesh,
        in_specs=(
            P(("long", "short"), None, None),
            P(("long", "short"), None, None),
            P(("long", "short"), None, None),
            P(None, None, ("long", "short")),
        ),
        out_specs=P(("long", "short"), None, None),
        check_vma=False,
    )
```

```python
import functools

import jax
import jax.numpy as jnp
from jax import lax
from jax.experimental import pallas as pl
from jax.experimental.pallas import tpu as pltpu
from jax.sharding import PartitionSpec as P

EPSILON = 1e-06
MIB = 1024 * 1024
NT = (((1,), (1,)), ((), ()))
NN = (((1,), (0,)), ((), ()))
RING = 4
CORES = 2
TILE = 256


def dot(lhs, rhs, dims):
    return lax.dot_general(lhs, rhs, dims, preferred_element_type=jnp.float32)


def params(mib):
    return pltpu.CompilerParams(vmem_limit_bytes=mib * MIB)


def cost(flops, mib):
    return pl.CostEstimate(flops=int(flops), bytes_accessed=int(mib * MIB), transcendentals=0)


def state_kernel(place_ref, key_ref, value_ref, state_ref, *quarter_refs):
    step = pl.program_id(0)

    @pl.when(step == 0)
    def _():
        state_ref[...] = jnp.zeros_like(state_ref)

    keys = jnp.swapaxes(key_ref[...], 0, 1)
    values = jnp.swapaxes(value_ref[...], 0, 1)
    heads = keys.shape[0]
    for head in range(heads):
        state_ref[head] += dot(values[head].T, keys[head], NN)

    @pl.when(step == pl.num_programs(0) - 1)
    def _():
        share = heads // RING
        for apart in range(RING):
            owner = place_ref[0] ^ apart
            quarter_refs[apart][...] = state_ref[pl.ds(owner * share, share)]


def states(place, key, value, rows=512):
    length, heads, width = key.shape
    share = heads // RING
    part = pl.BlockSpec((rows, heads, width), lambda i: (i, 0, 0))
    return pl.pallas_call(
        state_kernel,
        grid=(length // rows,),
        in_specs=[pl.BlockSpec(memory_space=pltpu.SMEM), part, part],
        out_specs=[pl.BlockSpec((heads, width, width), lambda i: (0, 0, 0))]
        + [pl.BlockSpec((share, width, width), lambda i: (0, 0, 0))] * RING,
        out_shape=[jax.ShapeDtypeStruct((heads, width, width), jnp.float32)]
        + [jax.ShapeDtypeStruct((share, width, width), jnp.float32)] * RING,
        compiler_params=params(60),
        cost_estimate=cost(3e8, 5),
        name="states",
    )(place, key, value)


def layout_kernel(query_ref, key_ref, value_ref, tie_ref, query_out, key_out, value_out):
    query_out[...] = jnp.swapaxes(query_ref[...], 0, 1)
    key_out[...] = jnp.swapaxes(key_ref[...], 0, 1)
    values = jnp.swapaxes(value_ref[...], 0, 1)
    for head in range(values.shape[0]):
        value_out[head] = values[head].T


def by_head(query, key, value, tie, rows=512):
    length, heads, width = query.shape
    part = pl.BlockSpec((rows, heads, width), lambda i: (i, 0, 0))
    rowwise = pl.BlockSpec((heads, rows, width), lambda i: (0, i, 0))
    return pl.pallas_call(
        layout_kernel,
        grid=(length // rows,),
        in_specs=[part] * 3 + [pl.BlockSpec(memory_space=pl.ANY)],
        out_specs=[rowwise, rowwise, pl.BlockSpec((heads, width, rows), lambda i: (0, 0, i))],
        out_shape=[jax.ShapeDtypeStruct((heads, length, width), jnp.bfloat16)] * 2
        + [jax.ShapeDtypeStruct((heads, width, length), jnp.bfloat16)],
        compiler_params=params(32),
        cost_estimate=cost(1e6, 12),
        name="by_head",
    )(query, key, value, tie)


def near_kernel(first, query_ref, key_ref, value_ref, weight_ref, tie_ref, near_ref):
    length = query_ref.shape[1]
    head = pl.program_id(0) + first
    groups = TILE // 8
    group_r = lax.broadcasted_iota(jnp.int32, (groups, TILE), 0)
    group_t = lax.broadcasted_iota(jnp.int32, (groups, TILE), 1) >> 3
    apart = group_r ^ group_t
    later = group_t > group_r
    inner_s = lax.broadcasted_iota(jnp.int32, (8, TILE), 0)
    inner_t = lax.broadcasted_iota(jnp.int32, (8, TILE), 1) & 7
    inner = inner_s ^ inner_t
    same = (
        lax.broadcasted_iota(jnp.int32, (groups, 8, TILE), 0)
        == lax.broadcasted_iota(jnp.int32, (groups, 8, TILE), 2) >> 3
    )
    for tile in range(length // TILE):
        cols = slice(tile * TILE, (tile + 1) * TILE)

        def gain(level):
            return weight_ref[level, pl.ds(head, 1), cols]

        query = query_ref[0, cols, :]
        parts = []
        for other in range(tile):
            scores = dot(key_ref[0, other * TILE : (other + 1) * TILE, :], query, NT)
            parts.append((scores * gain(8 + (tile ^ other).bit_length())).astype(jnp.bfloat16))
        outer = gain(4)
        for level in range(5, 9):
            outer = jnp.where(apart >= 1 << (level - 4), gain(level), outer)
        outer = jnp.where(later, outer, 0.0)
        small = gain(0)
        for level in range(1, 4):
            small = jnp.where(inner >= 1 << (level - 1), gain(level), small)
        small = jnp.where(inner_s <= inner_t, small, 0.0)
        mixing = jnp.where(same, small[None], outer[:, None, :]).reshape(TILE, TILE)
        scores = dot(key_ref[0, cols, :], query, NT)
        parts.append((scores * mixing).astype(jnp.bfloat16))
        weighted = jnp.concatenate(parts, 0)
        near_ref[0, :, cols] = dot(value_ref[0, :, : (tile + 1) * TILE], weighted, NN)


def near_part(query, key, value, level_weight, tie, first, count):
    heads, length, width = query.shape
    levels = level_weight.shape[0]
    rows = pl.BlockSpec((1, length, width), lambda h: (h + first, 0, 0))
    flat = pl.BlockSpec((1, width, length), lambda h: (h + first, 0, 0))
    return pl.pallas_call(
        functools.partial(near_kernel, first),
        grid=(count,),
        in_specs=[
            rows,
            rows,
            flat,
            pl.BlockSpec((levels, heads, length), lambda h: (0, 0, 0)),
            pl.BlockSpec(memory_space=pl.ANY),
        ],
        out_specs=pl.BlockSpec((1, width, length), lambda h: (h, 0, 0)),
        out_shape=jax.ShapeDtypeStruct((count, width, length), jnp.float32),
        compiler_params=params(16),
        cost_estimate=cost(count * 5e8, count * 2),
        name="near",
    )(query, key, value, level_weight, tie)


def far_kernel(plan, last, local_bits, place_ref, query_ref, weight_ref, *rest):
    count, bits, pieces = plan
    total_refs, rest = rest[:count], rest[count:]
    piece_refs, rest = rest[: len(pieces)], rest[len(pieces) :]
    if last:
        out_ref, split, total_f = rest
    else:
        out_ref, split = rest
    heads, rows, width = query_ref.shape

    @pl.when(pl.program_id(0) == 0)
    def _():
        for ref, (piece_bits, first_head) in zip(piece_refs, pieces):
            base = first_head(place_ref)
            for at, bit in enumerate(piece_bits):
                for head in range(ref.shape[1]):
                    bucket = ref[at, head]
                    high = bucket.astype(jnp.bfloat16)
                    low = (bucket - high.astype(jnp.float32)).astype(jnp.bfloat16)
                    where = bits.index(bit) * width
                    split[base + head, where : where + width, :width] = high
                    split[base + head, where : where + width, width:] = low

    block = place_ref[3]
    share = heads // count
    for head in range(heads):
        query = query_ref[head]
        products = dot(split[head], jnp.concatenate([query, query], 1), NT)
        total = total_refs[head // share][head % share]
        for at, bit in enumerate(bits):
            gain = weight_ref[local_bits + 1 + bit, head : head + 1, :]
            gain = jnp.where((block >> bit) & 1 == 1, gain, 0.0)
            total = total + products[at * width : (at + 1) * width, :] * gain
        if last:
            mean = jnp.sum(total * total, 0, keepdims=True) * (1.0 / width)
            total = total * lax.rsqrt(mean + EPSILON)
            total_f[pl.ds(head, rows, stride=heads), :] = total.T
        else:
            out_ref[head] = total
    if last:
        out_ref[...] = total_f[...].reshape(rows, heads, width).astype(jnp.bfloat16)


def far_part(place, query, level_weight, totals, bits, pieces, last, rows=256):
    heads, length, width = query.shape
    levels = level_weight.shape[0]
    local_bits = length.bit_length() - 1
    flat = pl.BlockSpec((heads, width, rows), lambda i: (0, 0, i))
    plan = (len(totals), bits, [(piece_bits, first) for _, piece_bits, first in pieces])
    arrays = [array for array, _, _ in pieces]
    scratch = [pltpu.VMEM((heads, len(bits) * width, 2 * width), jnp.bfloat16)]
    if last:
        scratch.append(pltpu.VMEM((rows * heads, width), jnp.float32))
    return pl.pallas_call(
        functools.partial(far_kernel, plan, last, local_bits),
        grid=(length // rows,),
        in_specs=[
            pl.BlockSpec(memory_space=pltpu.SMEM),
            pl.BlockSpec((heads, rows, width), lambda i: (0, i, 0)),
            pl.BlockSpec((levels, heads, rows), lambda i: (0, 0, i)),
        ]
        + [pl.BlockSpec((t.shape[0], width, rows), lambda i: (0, 0, i)) for t in totals]
        + [pl.BlockSpec(a.shape, lambda i: (0, 0, 0, 0)) for a in arrays],
        out_specs=pl.BlockSpec((rows, heads, width), lambda i: (i, 0, 0)) if last else flat,
        out_shape=jax.ShapeDtypeStruct((length, heads, width), jnp.bfloat16)
        if last
        else jax.ShapeDtypeStruct((heads, width, length), jnp.float32),
        scratch_shapes=scratch,
        compiler_params=params(28),
        cost_estimate=cost(len(bits) * 6e8, 10),
        name="finish" if last else "far",
    )(place, query, level_weight, *totals, *arrays)


def along(value, axis, hop):
    return lax.ppermute(value, axis, [(i, hop(i)) for i in range(lax.axis_size(axis))])


def apart_y(value, by):
    return along(value, "short", lambda i: i ^ by)


def apart_z(value, by):
    return along(value, "short", lambda i: i ^ by * RING)


def apart_x(value, by):
    return along(value, "long", lambda i: i ^ by * CORES)


def other_core(value):
    return along(value, "long", lambda i: i ^ 1)


def tied(value, *others):
    return lax.optimization_barrier((value, *others))[0]


def buckets_of_ring(parts):
    return parts[1], parts[2] + parts[3]


def per_device(query, key, value, level_weight):
    level_weight = jnp.transpose(level_weight, (1, 0, 2))
    short_pos = lax.axis_index("short").astype(jnp.int32)
    long_pos = lax.axis_index("long").astype(jnp.int32)
    y, core = short_pos % RING, long_pos % CORES
    block = long_pos * lax.axis_size("short") + short_pos
    place = jnp.stack([y, core, short_pos // RING, block])

    state, *quarters = states(place, key, value)
    quarters = [quarters[0]] + [apart_y(quarters[m], m) for m in (1, 3, 2)]
    quarters = [quarters[0], quarters[1], quarters[3], quarters[2]]
    first = apart_y(state, 1)
    query_h, key_h, value_t = by_head(query, key, value, quarters[0])
    heads = query_h.shape[0]
    share = heads // RING

    def near_of(head, tie):
        return near_part(query_h, key_h, value_t, level_weight, tie, head, share)

    quarters = tied(quarters, query_h)
    ring_y = sum(quarters[1:], quarters[0])

    sums = [ring_y] + [apart_z(ring_y, m) for m in (1, 2, 3)]
    near = [near_of(0, ring_y), near_of(share, ring_y)]
    sums, pair = lax.optimization_barrier((sums, state + first, *near))[:2]
    ring_z = sum(sums[1:], sums[0])
    second = apart_y(pair, 3)
    facing = other_core(ring_z)
    near_buckets = jnp.stack(buckets_of_ring(sums))

    mine = lax.dynamic_slice_in_dim(ring_z, core, 1, 0)
    theirs = lax.dynamic_slice_in_dim(facing, core, 1, 0)
    chip = mine + theirs
    chips = [chip] + [apart_x(chip, m) for m in (1, 2, 3)]
    near.append(near_of(2 * share, chip))
    near_buckets = tied(near_buckets, chip)
    inner = [near_buckets, apart_y(near_buckets, 1), None, apart_y(near_buckets, 3)]
    chips = tied(chips, near[2])
    outer = jnp.stack([jnp.where(core == 0, mine, theirs), *buckets_of_ring(chips)])
    outer = [outer] + [apart_y(outer, m) for m in (1, 2, 3)]
    inner[2] = apart_y(inner[1], 3)
    outer_facing = [other_core(piece) for piece in outer]
    near.append(near_of(3 * share, outer[0]))

    def owner(m):
        return lambda p: (p[0] ^ m) * share

    pieces = [(first[None], (0,), lambda p: 0), (second[None], (1,), lambda p: 0)]
    pieces += [(inner[m], (2, 3), owner(m)) for m in range(RING)]
    total = far_part(place, query_h, level_weight, near, (0, 1, 2, 3), pieces, False)
    pieces = [(outer[m], (4, 5, 6), lambda p, m=m: owner(m)(p) + p[1]) for m in range(RING)]
    pieces += [
        (outer_facing[m], (4, 5, 6), lambda p, m=m: owner(m)(p) + 1 - p[1]) for m in range(RING)
    ]
    return far_part(place, query_h, level_weight, [total], (4, 5, 6), pieces, True)


def solution(mesh):
    return jax.shard_map(
        per_device,
        mesh=mesh,
        in_specs=(
            P(("long", "short"), None, None),
            P(("long", "short"), None, None),
            P(("long", "short"), None, None),
            P(None, None, ("long", "short")),
        ),
        out_specs=P(("long", "short"), None, None),
        check_vma=False,
    )
```

```python
import functools

import jax
import jax.numpy as jnp
from jax import lax
from jax.experimental import pallas as pl
from jax.experimental.pallas import tpu as pltpu
from jax.sharding import PartitionSpec as P

EPSILON = 1e-06
MIB = 1024 * 1024
NT = (((1,), (1,)), ((), ()))
NN = (((1,), (0,)), ((), ()))
RING = 4
CORES = 2
TILE = 256
EARLY_HEADS = 4


def dot(lhs, rhs, dims):
    return lax.dot_general(lhs, rhs, dims, preferred_element_type=jnp.float32)


def params(mib):
    return pltpu.CompilerParams(vmem_limit_bytes=mib * MIB)


def cost(flops, mib):
    return pl.CostEstimate(flops=int(flops), bytes_accessed=int(mib * MIB), transcendentals=0)


def place():
    short_pos = lax.axis_index("short").astype(jnp.int32)
    long_pos = lax.axis_index("long").astype(jnp.int32)
    block = long_pos * lax.axis_size("short") + short_pos
    return short_pos & (RING - 1), long_pos & (CORES - 1), block


def state_kernel(key_ref, value_ref, state_ref, *quarter_refs):
    step = pl.program_id(0)

    @pl.when(step == 0)
    def _():
        state_ref[...] = jnp.zeros_like(state_ref)

    keys = jnp.swapaxes(key_ref[...], 0, 1)
    values = jnp.swapaxes(value_ref[...], 0, 1)
    heads = keys.shape[0]
    for head in range(heads):
        state_ref[head] += dot(values[head].T, keys[head], NN)

    @pl.when(step == pl.num_programs(0) - 1)
    def _():
        share = heads // RING
        for apart in range(RING):
            owner = place()[0] ^ apart
            quarter_refs[apart][...] = state_ref[pl.ds(owner * share, share)]


def states(key, value, rows=512):
    length, heads, width = key.shape
    share = heads // RING
    part = pl.BlockSpec((rows, heads, width), lambda i: (i, 0, 0))
    return pl.pallas_call(
        state_kernel,
        grid=(length // rows,),
        in_specs=[part, part],
        out_specs=[pl.BlockSpec((heads, width, width), lambda i: (0, 0, 0))]
        + [pl.BlockSpec((share, width, width), lambda i: (0, 0, 0))] * RING,
        out_shape=[jax.ShapeDtypeStruct((heads, width, width), jnp.float32)]
        + [jax.ShapeDtypeStruct((share, width, width), jnp.float32)] * RING,
        compiler_params=params(60),
        cost_estimate=cost(3e8, 5),
        name="states",
    )(key, value)


def layout_kernel(query_ref, key_ref, value_ref, query_out, key_out, value_out):
    query_out[...] = jnp.swapaxes(query_ref[...], 0, 1)
    key_out[...] = jnp.swapaxes(key_ref[...], 0, 1)
    values = jnp.swapaxes(value_ref[...], 0, 1)
    for head in range(values.shape[0]):
        value_out[head] = values[head].T


def by_head(query, key, value, rows=512):
    length, heads, width = query.shape
    part = pl.BlockSpec((rows, heads, width), lambda i: (i, 0, 0))
    rowwise = pl.BlockSpec((heads, rows, width), lambda i: (0, i, 0))
    return pl.pallas_call(
        layout_kernel,
        grid=(length // rows,),
        in_specs=[part] * 3,
        out_specs=[rowwise, rowwise, pl.BlockSpec((heads, width, rows), lambda i: (0, 0, i))],
        out_shape=[jax.ShapeDtypeStruct((heads, length, width), jnp.bfloat16)] * 2
        + [jax.ShapeDtypeStruct((heads, width, length), jnp.bfloat16)],
        compiler_params=params(24),
        cost_estimate=cost(1e6, 0.01),
        name="by_head",
    )(query, key, value)


def near_kernel(first, query_ref, key_ref, value_ref, weight_ref, tie_ref, near_ref):
    length = query_ref.shape[1]
    head = pl.program_id(0) + first
    groups = TILE // 8
    group_r = lax.broadcasted_iota(jnp.int32, (groups, TILE), 0)
    group_t = lax.broadcasted_iota(jnp.int32, (groups, TILE), 1) >> 3
    apart = group_r ^ group_t
    later = group_t > group_r
    inner_s = lax.broadcasted_iota(jnp.int32, (8, TILE), 0)
    inner_t = lax.broadcasted_iota(jnp.int32, (8, TILE), 1) & 7
    inner = inner_s ^ inner_t
    same = (
        lax.broadcasted_iota(jnp.int32, (groups, 8, TILE), 0)
        == lax.broadcasted_iota(jnp.int32, (groups, 8, TILE), 2) >> 3
    )
    for tile in range(length // TILE):
        cols = slice(tile * TILE, (tile + 1) * TILE)

        def gain(level):
            return weight_ref[level, pl.ds(head, 1), cols]

        query = query_ref[0, cols, :]
        parts = []
        for other in range(tile):
            scores = dot(key_ref[0, other * TILE : (other + 1) * TILE, :], query, NT)
            parts.append((scores * gain(8 + (tile ^ other).bit_length())).astype(jnp.bfloat16))
        outer = gain(4)
        for level in range(5, 9):
            outer = jnp.where(apart >= 1 << (level - 4), gain(level), outer)
        outer = jnp.where(later, outer, 0.0)
        small = gain(0)
        for level in range(1, 4):
            small = jnp.where(inner >= 1 << (level - 1), gain(level), small)
        small = jnp.where(inner_s <= inner_t, small, 0.0)
        mixing = jnp.where(same, small[None], outer[:, None, :]).reshape(TILE, TILE)
        scores = dot(key_ref[0, cols, :], query, NT)
        parts.append((scores * mixing).astype(jnp.bfloat16))
        weighted = jnp.concatenate(parts, 0)
        near_ref[0, :, cols] = dot(value_ref[0, :, : (tile + 1) * TILE], weighted, NN)


def near_part(query, key, value, level_weight, tie, first, count, mib):
    heads, length, width = query.shape
    levels = level_weight.shape[0]
    rows = pl.BlockSpec((1, length, width), lambda h: (h + first, 0, 0))
    flat = pl.BlockSpec((1, width, length), lambda h: (h + first, 0, 0))
    return pl.pallas_call(
        functools.partial(near_kernel, first),
        grid=(count,),
        in_specs=[
            rows,
            rows,
            flat,
            pl.BlockSpec((levels, heads, length), lambda h: (0, 0, 0)),
            pl.BlockSpec(memory_space=pl.ANY),
        ],
        out_specs=pl.BlockSpec((1, width, length), lambda h: (h, 0, 0)),
        out_shape=jax.ShapeDtypeStruct((count, width, length), jnp.float32),
        compiler_params=params(mib),
        cost_estimate=cost(1e6, 0.01),
        name="near",
    )(query, key, value, level_weight, tie)


def far_kernel(plan, last, local_bits, query_ref, weight_ref, *rest):
    count, bits, pieces = plan
    total_refs, rest = rest[:count], rest[count:]
    piece_refs, rest = rest[: len(pieces)], rest[len(pieces) :]
    if last:
        out_ref, split, total_f = rest
    else:
        out_ref, split = rest
    heads, rows, width = query_ref.shape

    @pl.when(pl.program_id(0) == 0)
    def _():
        for ref, (piece_bits, first_head) in zip(piece_refs, pieces):
            base = first_head(place())
            for at, bit in enumerate(piece_bits):
                for head in range(ref.shape[1]):
                    bucket = ref[at, head]
                    high = bucket.astype(jnp.bfloat16)
                    low = (bucket - high.astype(jnp.float32)).astype(jnp.bfloat16)
                    where = bits.index(bit) * width
                    split[base + head, where : where + width, :width] = high
                    split[base + head, where : where + width, width:] = low

    block = place()[2]
    held = [(ref, at) for ref in total_refs for at in range(ref.shape[0])]
    for head in range(heads):
        query = query_ref[head]
        products = dot(split[head], jnp.concatenate([query, query], 1), NT)
        ref, at = held[head]
        total = ref[at]
        for at, bit in enumerate(bits):
            gain = weight_ref[local_bits + 1 + bit, head : head + 1, :]
            gain = jnp.where((block >> bit) & 1 == 1, gain, 0.0)
            total = total + products[at * width : (at + 1) * width, :] * gain
        if last:
            mean = jnp.sum(total * total, 0, keepdims=True) * (1.0 / width)
            total = total * lax.rsqrt(mean + EPSILON)
            total_f[pl.ds(head, rows, stride=heads), :] = total.T
        else:
            out_ref[head] = total
    if last:
        out_ref[...] = total_f[...].reshape(rows, heads, width).astype(jnp.bfloat16)


def far_part(query, level_weight, totals, bits, pieces, last, rows=512):
    heads, length, width = query.shape
    levels = level_weight.shape[0]
    local_bits = length.bit_length() - 1
    flat = pl.BlockSpec((heads, width, rows), lambda i: (0, 0, i))
    plan = (len(totals), bits, [(piece_bits, first) for _, piece_bits, first in pieces])
    arrays = [array for array, _, _ in pieces]
    scratch = [pltpu.VMEM((heads, len(bits) * width, 2 * width), jnp.bfloat16)]
    if last:
        scratch.append(pltpu.VMEM((rows * heads, width), jnp.float32))
    return pl.pallas_call(
        functools.partial(far_kernel, plan, last, local_bits),
        grid=(length // rows,),
        in_specs=[
            pl.BlockSpec((heads, rows, width), lambda i: (0, i, 0)),
            pl.BlockSpec((levels, heads, rows), lambda i: (0, 0, i)),
        ]
        + [pl.BlockSpec((t.shape[0], width, rows), lambda i: (0, 0, i)) for t in totals]
        + [pl.BlockSpec(a.shape, lambda i: (0, 0, 0, 0)) for a in arrays],
        out_specs=pl.BlockSpec((rows, heads, width), lambda i: (i, 0, 0)) if last else flat,
        out_shape=jax.ShapeDtypeStruct((length, heads, width), jnp.bfloat16)
        if last
        else jax.ShapeDtypeStruct((heads, width, length), jnp.float32),
        scratch_shapes=scratch,
        compiler_params=params(20 if last else 24),
        cost_estimate=cost(1e6, 0.01),
        name="finish" if last else "far",
    )(query, level_weight, *totals, *arrays)


def along(value, axis, hop):
    return lax.ppermute(value, axis, [(i, hop(i)) for i in range(lax.axis_size(axis))])


def apart_y(value, by):
    return along(value, "short", lambda i: i ^ by)


def apart_z(value, by):
    return along(value, "short", lambda i: i ^ by * RING)


def apart_x(value, by):
    return along(value, "long", lambda i: i ^ by * CORES)


def other_core(value):
    return along(value, "long", lambda i: i ^ 1)


def tied(value, *others):
    return lax.optimization_barrier((value, *others))[0]


def buckets_of_ring(parts):
    return parts[1], parts[2] + parts[3]


def per_device(query, key, value, level_weight):
    level_weight = jnp.transpose(level_weight, (1, 0, 2))
    core = place()[1]
    state, *quarters = states(key, value)
    quarters = [quarters[0]] + [apart_y(quarters[m], m) for m in (1, 2, 3)]
    query_h, key_h, value_t = by_head(tied(query, state), key, value)
    first = apart_y(state, 1)
    heads = query_h.shape[0]
    share = heads // RING

    quarters = tied(quarters, query_h)
    ring_y = sum(quarters[1:], quarters[0])

    def near_of(head, count, tie, mib):
        return near_part(query_h, key_h, value_t, level_weight, tie, head, count, mib)

    sums = [ring_y] + [apart_z(ring_y, m) for m in (1, 2, 3)]
    near = [near_of(0, EARLY_HEADS, ring_y, 12)]
    sums = tied(sums, near[0])
    ring_z = sum(sums[1:], sums[0])
    facing = other_core(ring_z)
    pair = state + tied(first, ring_z)
    second = apart_y(pair, 3)
    facing = tied(facing, pair)
    near_buckets = jnp.stack(buckets_of_ring(sums))
    inner = [near_buckets, apart_y(near_buckets, 1), None, None]

    mine = lax.dynamic_slice_in_dim(ring_z, core, 1, 0)
    theirs = lax.dynamic_slice_in_dim(facing, core, 1, 0)
    chip = mine + theirs
    chip_first = apart_x(chip, 1)
    inner[3] = apart_y(tied(near_buckets, chip), 3)
    chip_second = apart_x(chip + chip_first, 3)
    chip_second = tied(chip_second, inner[1], inner[3])
    outer = jnp.stack([jnp.where(core == 0, mine, theirs), chip_first, chip_second])
    outer_facing = [other_core(outer)]
    outer = [outer] + [apart_y(outer, m) for m in (1, 2, 3)]
    inner[2] = apart_y(tied(inner[3], outer_facing[0]), 1)
    near.append(near_of(EARLY_HEADS, heads - EARLY_HEADS, outer_facing[0], 12))

    def owner(m):
        return lambda p: (p[0] ^ m) * share

    pieces = [(first[None], (0,), lambda p: 0), (second[None], (1,), lambda p: 0)]
    pieces += [(inner[m], (2, 3), owner(m)) for m in range(RING)]
    total = far_part(query_h, level_weight, near, (0, 1, 2, 3), pieces, False)
    outer = [outer[0]] + tied(outer[1:], total)
    outer_facing += [other_core(piece) for piece in outer[1:]]
    pieces = [(outer[m], (4, 5, 6), lambda p, m=m: owner(m)(p) + p[1]) for m in range(RING)]
    pieces += [
        (outer_facing[m], (4, 5, 6), lambda p, m=m: owner(m)(p) + 1 - p[1]) for m in range(RING)
    ]
    return far_part(query_h, level_weight, [total], (4, 5, 6), pieces, True)


def solution(mesh):
    return jax.shard_map(
        per_device,
        mesh=mesh,
        in_specs=(
            P(("long", "short"), None, None),
            P(("long", "short"), None, None),
            P(("long", "short"), None, None),
            P(None, None, ("long", "short")),
        ),
        out_specs=P(("long", "short"), None, None),
        check_vma=False,
    )
```

```python
import functools

import jax
import jax.numpy as jnp
from jax import lax
from jax.experimental import pallas as pl
from jax.experimental.pallas import tpu as pltpu
from jax.sharding import PartitionSpec as P

EPSILON = 1e-06
MIB = 1024 * 1024
NT = (((1,), (1,)), ((), ()))
NN = (((1,), (0,)), ((), ()))
RING = 4
CORES = 2
TILE = 256
EARLY_HEADS = 3
ROWS = 512


def dot(lhs, rhs, dims):
    return lax.dot_general(lhs, rhs, dims, preferred_element_type=jnp.float32)


def params(mib):
    return pltpu.CompilerParams(vmem_limit_bytes=mib * MIB)


def cost(flops, mib):
    return pl.CostEstimate(flops=int(flops), bytes_accessed=int(mib * MIB), transcendentals=0)


def place():
    short_pos = lax.axis_index("short").astype(jnp.int32)
    long_pos = lax.axis_index("long").astype(jnp.int32)
    block = long_pos * lax.axis_size("short") + short_pos
    return short_pos & (RING - 1), long_pos & (CORES - 1), block


def state_kernel(key_ref, value_ref, state_ref, *quarter_refs):
    step = pl.program_id(0)

    @pl.when(step == 0)
    def _():
        state_ref[...] = jnp.zeros_like(state_ref)

    keys = jnp.swapaxes(key_ref[...], 0, 1)
    values = jnp.swapaxes(value_ref[...], 0, 1)
    heads = keys.shape[0]
    for head in range(heads):
        state_ref[head] += dot(values[head].T, keys[head], NN)

    @pl.when(step == pl.num_programs(0) - 1)
    def _():
        share = heads // RING
        for apart in range(RING):
            owner = place()[0] ^ apart
            quarter_refs[apart][...] = state_ref[pl.ds(owner * share, share)]


def states(key, value, rows=512):
    length, heads, width = key.shape
    share = heads // RING
    part = pl.BlockSpec((rows, heads, width), lambda i: (i, 0, 0))
    return pl.pallas_call(
        state_kernel,
        grid=(length // rows,),
        in_specs=[part, part],
        out_specs=[pl.BlockSpec((heads, width, width), lambda i: (0, 0, 0))]
        + [pl.BlockSpec((share, width, width), lambda i: (0, 0, 0))] * RING,
        out_shape=[jax.ShapeDtypeStruct((heads, width, width), jnp.float32)]
        + [jax.ShapeDtypeStruct((share, width, width), jnp.float32)] * RING,
        compiler_params=params(60),
        cost_estimate=cost(3e8, 5),
        name="states",
    )(key, value)


def layout_kernel(query_ref, key_ref, value_ref, query_out, key_out, value_out):
    query_out[...] = jnp.swapaxes(query_ref[...], 0, 1)
    key_out[...] = jnp.swapaxes(key_ref[...], 0, 1)
    values = jnp.swapaxes(value_ref[...], 0, 1)
    for head in range(values.shape[0]):
        value_out[head] = values[head].T


def by_head(query, key, value, rows=512):
    length, heads, width = query.shape
    part = pl.BlockSpec((rows, heads, width), lambda i: (i, 0, 0))
    rowwise = pl.BlockSpec((heads, rows, width), lambda i: (0, i, 0))
    return pl.pallas_call(
        layout_kernel,
        grid=(length // rows,),
        in_specs=[part] * 3,
        out_specs=[rowwise, rowwise, pl.BlockSpec((heads, width, rows), lambda i: (0, 0, i))],
        out_shape=[jax.ShapeDtypeStruct((heads, length, width), jnp.bfloat16)] * 2
        + [jax.ShapeDtypeStruct((heads, width, length), jnp.bfloat16)],
        compiler_params=params(24),
        cost_estimate=cost(1e6, 0.01),
        name="by_head",
    )(query, key, value)


def near_kernel(first, query_ref, key_ref, value_ref, weight_ref, tie_ref, near_ref):
    length = query_ref.shape[1]
    head = pl.program_id(0) + first
    groups = TILE // 8
    group_r = lax.broadcasted_iota(jnp.int32, (groups, TILE), 0)
    group_t = lax.broadcasted_iota(jnp.int32, (groups, TILE), 1) >> 3
    apart = group_r ^ group_t
    later = group_t > group_r
    inner_s = lax.broadcasted_iota(jnp.int32, (8, TILE), 0)
    inner_t = lax.broadcasted_iota(jnp.int32, (8, TILE), 1) & 7
    inner = inner_s ^ inner_t
    same = (
        lax.broadcasted_iota(jnp.int32, (groups, 8, TILE), 0)
        == lax.broadcasted_iota(jnp.int32, (groups, 8, TILE), 2) >> 3
    )
    for tile in range(length // TILE):
        cols = slice(tile * TILE, (tile + 1) * TILE)

        def gain(level):
            return weight_ref[level, pl.ds(head, 1), cols]

        query = query_ref[0, cols, :]
        parts = []
        for other in range(tile):
            scores = dot(key_ref[0, other * TILE : (other + 1) * TILE, :], query, NT)
            parts.append((scores * gain(8 + (tile ^ other).bit_length())).astype(jnp.bfloat16))
        outer = gain(4)
        for level in range(5, 9):
            outer = jnp.where(apart >= 1 << (level - 4), gain(level), outer)
        outer = jnp.where(later, outer, 0.0)
        small = gain(0)
        for level in range(1, 4):
            small = jnp.where(inner >= 1 << (level - 1), gain(level), small)
        small = jnp.where(inner_s <= inner_t, small, 0.0)
        mixing = jnp.where(same, small[None], outer[:, None, :]).reshape(TILE, TILE)
        scores = dot(key_ref[0, cols, :], query, NT)
        parts.append((scores * mixing).astype(jnp.bfloat16))
        weighted = jnp.concatenate(parts, 0)
        near_ref[0, :, cols] = dot(value_ref[0, :, : (tile + 1) * TILE], weighted, NN)


def near_part(query, key, value, level_weight, tie, first, count, mib):
    heads, length, width = query.shape
    levels = level_weight.shape[0]
    rows = pl.BlockSpec((1, length, width), lambda h: (h + first, 0, 0))
    flat = pl.BlockSpec((1, width, length), lambda h: (h + first, 0, 0))
    return pl.pallas_call(
        functools.partial(near_kernel, first),
        grid=(count,),
        in_specs=[
            rows,
            rows,
            flat,
            pl.BlockSpec((levels, heads, length), lambda h: (0, 0, 0)),
            pl.BlockSpec(memory_space=pl.ANY),
        ],
        out_specs=pl.BlockSpec((1, width, length), lambda h: (h, 0, 0)),
        out_shape=jax.ShapeDtypeStruct((count, width, length), jnp.float32),
        compiler_params=params(mib),
        cost_estimate=cost(1e6, 0.01),
        name="near",
    )(query, key, value, level_weight, tie)


def far_kernel(plan, last, local_bits, query_ref, weight_ref, *rest):
    count, bits, pieces = plan
    total_refs, rest = rest[:count], rest[count:]
    piece_refs, rest = rest[: len(pieces)], rest[len(pieces) :]
    if last:
        out_ref, split, result, sent = rest
    else:
        out_ref, split = rest
    heads, length, width = query_ref.shape
    for ref, (piece_bits, first_head) in zip(piece_refs, pieces):
        base = first_head(place())
        for at, bit in enumerate(piece_bits):
            for head in range(ref.shape[1]):
                bucket = ref[at, head]
                high = bucket.astype(jnp.bfloat16)
                low = (bucket - high.astype(jnp.float32)).astype(jnp.bfloat16)
                where = bits.index(bit) * width
                split[base + head, where : where + width, :width] = high
                split[base + head, where : where + width, width:] = low

    block = place()[2]
    held = [(ref, at) for ref in total_refs for at in range(ref.shape[0])]
    copies = []
    for start in range(0, length, ROWS):
        cols = slice(start, start + ROWS)
        done = []
        for head in range(heads):
            query = query_ref[head, cols, :]
            products = dot(split[head], jnp.concatenate([query, query], 1), NT)
            ref, at = held[head]
            total = ref[at, :, cols]
            for at, bit in enumerate(bits):
                gain = weight_ref[local_bits + 1 + bit, head : head + 1, cols]
                gain = jnp.where((block >> bit) & 1 == 1, gain, 0.0)
                total = total + products[at * width : (at + 1) * width, :] * gain
            if last:
                mean = jnp.sum(total * total, 0, keepdims=True) * (1.0 / width)
                done.append((total * lax.rsqrt(mean + EPSILON)).astype(jnp.bfloat16).T)
            else:
                out_ref[head, :, cols] = total
        if last:
            result[cols] = jnp.swapaxes(jnp.stack(done), 0, 1)
            copies.append(
                pltpu.make_async_copy(result.at[cols], out_ref.at[cols], sent.at[len(copies)])
            )
            copies[-1].start()
    for copy in copies:
        copy.wait()


def far_part(query, level_weight, totals, bits, pieces, last):
    heads, length, width = query.shape
    local_bits = length.bit_length() - 1
    plan = (len(totals), bits, [(piece_bits, first) for _, piece_bits, first in pieces])
    arrays = [array for array, _, _ in pieces]
    scratch = [pltpu.VMEM((heads, len(bits) * width, 2 * width), jnp.bfloat16)]
    if last:
        scratch.append(pltpu.VMEM((length, heads, width), jnp.bfloat16))
        scratch.append(pltpu.SemaphoreType.DMA((length // ROWS,)))
    held = pl.BlockSpec(memory_space=pltpu.VMEM)
    return pl.pallas_call(
        functools.partial(far_kernel, plan, last, local_bits),
        in_specs=[held] * (2 + len(totals) + len(arrays)),
        out_specs=pl.BlockSpec(memory_space=pl.ANY) if last else held,
        out_shape=jax.ShapeDtypeStruct((length, heads, width), jnp.bfloat16)
        if last
        else jax.ShapeDtypeStruct((heads, width, length), jnp.float32),
        scratch_shapes=scratch,
        compiler_params=params(24),
        cost_estimate=cost(1e6, 0.01),
        name="finish" if last else "far",
    )(query, level_weight, *totals, *arrays)


def along(value, axis, hop):
    return lax.ppermute(value, axis, [(i, hop(i)) for i in range(lax.axis_size(axis))])


def apart_y(value, by):
    return along(value, "short", lambda i: i ^ by)


def apart_z(value, by):
    return along(value, "short", lambda i: i ^ by * RING)


def apart_x(value, by):
    return along(value, "long", lambda i: i ^ by * CORES)


def other_core(value):
    return along(value, "long", lambda i: i ^ 1)


def tied(value, *others):
    return lax.optimization_barrier((value, *others))[0]


def buckets_of_ring(parts):
    return parts[1], parts[2] + parts[3]


def per_device(query, key, value, level_weight):
    level_weight = jnp.transpose(level_weight, (1, 0, 2))
    core = place()[1]
    state, *quarters = states(key, value)
    quarters = [quarters[0]] + [apart_y(quarters[m], m) for m in (1, 2, 3)]
    query_h, key_h, value_t = by_head(tied(query, state), key, value)
    first = apart_y(state, 1)
    heads = query_h.shape[0]
    share = heads // RING

    quarters = tied(quarters, query_h)
    ring_y = sum(quarters[1:], quarters[0])

    def near_of(head, count, tie, mib):
        return near_part(query_h, key_h, value_t, level_weight, tie, head, count, mib)

    sums = [ring_y] + [apart_z(ring_y, m) for m in (1, 2, 3)]
    near = [near_of(0, EARLY_HEADS, ring_y, 12)]
    sums = tied(sums, near[0])
    ring_z = sum(sums[1:], sums[0])
    facing = other_core(ring_z)
    pair = state + tied(first, ring_z)
    second = apart_y(pair, 3)
    facing = tied(facing, pair)
    near_buckets = jnp.stack(buckets_of_ring(sums))
    inner = [near_buckets, apart_y(near_buckets, 1), None, None]

    mine = lax.dynamic_slice_in_dim(ring_z, core, 1, 0)
    theirs = lax.dynamic_slice_in_dim(facing, core, 1, 0)
    chip = mine + theirs
    chip_first = apart_x(chip, 1)
    inner[3] = apart_y(tied(near_buckets, chip), 3)
    chip_second = apart_x(chip + chip_first, 3)
    chip_second = tied(chip_second, inner[1], inner[3])
    outer = jnp.stack([jnp.where(core == 0, mine, theirs), chip_first, chip_second])
    outer = [outer] + [apart_y(outer, m) for m in (1, 2, 3)]
    inner[2] = apart_y(inner[3], 1)
    near.append(near_of(EARLY_HEADS, heads - EARLY_HEADS, outer[0], 12))

    def owner(m):
        return lambda p: (p[0] ^ m) * share

    pieces = [(first[None], (0,), lambda p: 0), (second[None], (1,), lambda p: 0)]
    pieces += [(inner[m], (2, 3), owner(m)) for m in range(RING)]
    total = far_part(query_h, level_weight, near, (0, 1, 2, 3), pieces, False)
    outer = tied(outer, total)
    outer_facing = [other_core(piece) for piece in outer]
    pieces = [(outer[m], (4, 5, 6), lambda p, m=m: owner(m)(p) + p[1]) for m in range(RING)]
    pieces += [
        (outer_facing[m], (4, 5, 6), lambda p, m=m: owner(m)(p) + 1 - p[1]) for m in range(RING)
    ]
    return far_part(query_h, level_weight, [total], (4, 5, 6), pieces, True)


def solution(mesh):
    return jax.shard_map(
        per_device,
        mesh=mesh,
        in_specs=(
            P(("long", "short"), None, None),
            P(("long", "short"), None, None),
            P(("long", "short"), None, None),
            P(None, None, ("long", "short")),
        ),
        out_specs=P(("long", "short"), None, None),
        check_vma=False,
    )
```

```python
import functools

import jax
import jax.numpy as jnp
from jax import lax
from jax.experimental import pallas as pl
from jax.experimental.pallas import tpu as pltpu
from jax.sharding import PartitionSpec as P

EPSILON = 1e-06
MIB = 1024 * 1024
NT = (((1,), (1,)), ((), ()))
NN = (((1,), (0,)), ((), ()))
RING = 4
CORES = 2
TILE = 256
EARLY_HEADS = 4
ROWS = 512


def dot(lhs, rhs, dims):
    return lax.dot_general(lhs, rhs, dims, preferred_element_type=jnp.float32)


def params(mib):
    return pltpu.CompilerParams(vmem_limit_bytes=mib * MIB)


def cost(flops, mib):
    return pl.CostEstimate(flops=int(flops), bytes_accessed=int(mib * MIB), transcendentals=0)


def place():
    short_pos = lax.axis_index("short").astype(jnp.int32)
    long_pos = lax.axis_index("long").astype(jnp.int32)
    block = long_pos * lax.axis_size("short") + short_pos
    return short_pos & (RING - 1), long_pos & (CORES - 1), block


def state_kernel(key_ref, value_ref, state_ref, *quarter_refs):
    step = pl.program_id(0)

    @pl.when(step == 0)
    def _():
        state_ref[...] = jnp.zeros_like(state_ref)

    keys = jnp.swapaxes(key_ref[...], 0, 1)
    values = jnp.swapaxes(value_ref[...], 0, 1)
    heads = keys.shape[0]
    for head in range(heads):
        state_ref[head] += dot(values[head].T, keys[head], NN)

    @pl.when(step == pl.num_programs(0) - 1)
    def _():
        share = heads // RING
        for apart in range(RING):
            owner = place()[0] ^ apart
            quarter_refs[apart][...] = state_ref[pl.ds(owner * share, share)]


def states(key, value, rows=512):
    length, heads, width = key.shape
    share = heads // RING
    part = pl.BlockSpec((rows, heads, width), lambda i: (i, 0, 0))
    return pl.pallas_call(
        state_kernel,
        grid=(length // rows,),
        in_specs=[part, part],
        out_specs=[pl.BlockSpec((heads, width, width), lambda i: (0, 0, 0))]
        + [pl.BlockSpec((share, width, width), lambda i: (0, 0, 0))] * RING,
        out_shape=[jax.ShapeDtypeStruct((heads, width, width), jnp.float32)]
        + [jax.ShapeDtypeStruct((share, width, width), jnp.float32)] * RING,
        compiler_params=params(60),
        cost_estimate=cost(3e8, 5),
        name="states",
    )(key, value)


def layout_kernel(query_ref, key_ref, value_ref, query_out, key_out, value_out):
    query_out[...] = jnp.swapaxes(query_ref[...], 0, 1)
    key_out[...] = jnp.swapaxes(key_ref[...], 0, 1)
    values = jnp.swapaxes(value_ref[...], 0, 1)
    for head in range(values.shape[0]):
        value_out[head] = values[head].T


def by_head(query, key, value, rows=512):
    length, heads, width = query.shape
    part = pl.BlockSpec((rows, heads, width), lambda i: (i, 0, 0))
    rowwise = pl.BlockSpec((heads, rows, width), lambda i: (0, i, 0))
    return pl.pallas_call(
        layout_kernel,
        grid=(length // rows,),
        in_specs=[part] * 3,
        out_specs=[rowwise, rowwise, pl.BlockSpec((heads, width, rows), lambda i: (0, 0, i))],
        out_shape=[jax.ShapeDtypeStruct((heads, length, width), jnp.bfloat16)] * 2
        + [jax.ShapeDtypeStruct((heads, width, length), jnp.bfloat16)],
        compiler_params=params(24),
        cost_estimate=cost(1e6, 0.01),
        name="by_head",
    )(query, key, value)


def near_kernel(first, query_ref, key_ref, value_ref, weight_ref, tie_ref, near_ref):
    length = query_ref.shape[1]
    head = pl.program_id(0) + first
    groups = TILE // 8
    group_r = lax.broadcasted_iota(jnp.int32, (groups, TILE), 0)
    group_t = lax.broadcasted_iota(jnp.int32, (groups, TILE), 1) >> 3
    apart = group_r ^ group_t
    later = group_t > group_r
    inner_s = lax.broadcasted_iota(jnp.int32, (8, TILE), 0)
    inner_t = lax.broadcasted_iota(jnp.int32, (8, TILE), 1) & 7
    inner = inner_s ^ inner_t
    same = (
        lax.broadcasted_iota(jnp.int32, (groups, 8, TILE), 0)
        == lax.broadcasted_iota(jnp.int32, (groups, 8, TILE), 2) >> 3
    )
    for tile in range(length // TILE):
        cols = slice(tile * TILE, (tile + 1) * TILE)

        def gain(level):
            return weight_ref[level, pl.ds(head, 1), cols]

        query = query_ref[0, cols, :]
        parts = []
        for other in range(tile):
            scores = dot(key_ref[0, other * TILE : (other + 1) * TILE, :], query, NT)
            parts.append((scores * gain(8 + (tile ^ other).bit_length())).astype(jnp.bfloat16))
        outer = gain(4)
        for level in range(5, 9):
            outer = jnp.where(apart >= 1 << (level - 4), gain(level), outer)
        outer = jnp.where(later, outer, 0.0)
        small = gain(0)
        for level in range(1, 4):
            small = jnp.where(inner >= 1 << (level - 1), gain(level), small)
        small = jnp.where(inner_s <= inner_t, small, 0.0)
        mixing = jnp.where(same, small[None], outer[:, None, :]).reshape(TILE, TILE)
        scores = dot(key_ref[0, cols, :], query, NT)
        parts.append((scores * mixing).astype(jnp.bfloat16))
        weighted = jnp.concatenate(parts, 0)
        near_ref[0, :, cols] = dot(value_ref[0, :, : (tile + 1) * TILE], weighted, NN)


def near_part(query, key, value, level_weight, tie, first, count, mib):
    heads, length, width = query.shape
    levels = level_weight.shape[0]
    rows = pl.BlockSpec((1, length, width), lambda h: (h + first, 0, 0))
    flat = pl.BlockSpec((1, width, length), lambda h: (h + first, 0, 0))
    return pl.pallas_call(
        functools.partial(near_kernel, first),
        grid=(count,),
        in_specs=[
            rows,
            rows,
            flat,
            pl.BlockSpec((levels, heads, length), lambda h: (0, 0, 0)),
            pl.BlockSpec(memory_space=pl.ANY),
        ],
        out_specs=pl.BlockSpec((1, width, length), lambda h: (h, 0, 0)),
        out_shape=jax.ShapeDtypeStruct((count, width, length), jnp.float32),
        compiler_params=params(mib),
        cost_estimate=cost(1e6, 0.01),
        name="near",
    )(query, key, value, level_weight, tie)


def far_kernel(plan, last, local_bits, query_ref, weight_ref, *rest):
    count, bits, pieces = plan
    total_refs, rest = rest[:count], rest[count:]
    piece_refs, rest = rest[: len(pieces)], rest[len(pieces) :]
    if last:
        out_ref, split, result, sent = rest
    else:
        out_ref, split = rest
    heads, length, width = query_ref.shape
    for ref, (piece_bits, first_head) in zip(piece_refs, pieces):
        base = first_head(place())
        for at, bit in enumerate(piece_bits):
            for head in range(ref.shape[1]):
                bucket = ref[at, head]
                high = bucket.astype(jnp.bfloat16)
                low = (bucket - high.astype(jnp.float32)).astype(jnp.bfloat16)
                where = bits.index(bit) * width
                split[base + head, where : where + width, :width] = high
                split[base + head, where : where + width, width:] = low

    block = place()[2]
    held = [(ref, at) for ref in total_refs for at in range(ref.shape[0])]
    copies = []
    rows = ROWS // 2 if last else ROWS
    for start in range(0, length, rows):
        cols = slice(start, start + rows)
        done = []
        for head in range(heads):
            query = query_ref[head, cols, :]
            products = dot(split[head], jnp.concatenate([query, query], 1), NT)
            ref, at = held[head]
            total = ref[at, :, cols]
            for at, bit in enumerate(bits):
                gain = weight_ref[local_bits + 1 + bit, head : head + 1, cols]
                gain = jnp.where((block >> bit) & 1 == 1, gain, 0.0)
                total = total + products[at * width : (at + 1) * width, :] * gain
            if last:
                mean = jnp.sum(total * total, 0, keepdims=True) * (1.0 / width)
                done.append((total * lax.rsqrt(mean + EPSILON)).astype(jnp.bfloat16).T)
            else:
                out_ref[head, :, cols] = total
        if last:
            result[cols] = jnp.swapaxes(jnp.stack(done), 0, 1)
            copies.append(
                pltpu.make_async_copy(result.at[cols], out_ref.at[cols], sent.at[len(copies)])
            )
            copies[-1].start()
    for copy in copies:
        copy.wait()


def far_part(query, level_weight, totals, bits, pieces, last):
    heads, length, width = query.shape
    local_bits = length.bit_length() - 1
    plan = (len(totals), bits, [(piece_bits, first) for _, piece_bits, first in pieces])
    arrays = [array for array, _, _ in pieces]
    scratch = [pltpu.VMEM((heads, len(bits) * width, 2 * width), jnp.bfloat16)]
    if last:
        scratch.append(pltpu.VMEM((length, heads, width), jnp.bfloat16))
        scratch.append(pltpu.SemaphoreType.DMA((2 * length // ROWS,)))
    held = pl.BlockSpec(memory_space=pltpu.VMEM)
    return pl.pallas_call(
        functools.partial(far_kernel, plan, last, local_bits),
        in_specs=[held] * (2 + len(totals) + len(arrays)),
        out_specs=pl.BlockSpec(memory_space=pl.ANY) if last else held,
        out_shape=jax.ShapeDtypeStruct((length, heads, width), jnp.bfloat16)
        if last
        else jax.ShapeDtypeStruct((heads, width, length), jnp.float32),
        scratch_shapes=scratch,
        compiler_params=params(24),
        cost_estimate=cost(1e6, 0.01),
        name="finish" if last else "far",
    )(query, level_weight, *totals, *arrays)


def along(value, axis, hop):
    return lax.ppermute(value, axis, [(i, hop(i)) for i in range(lax.axis_size(axis))])


def apart_y(value, by):
    return along(value, "short", lambda i: i ^ by)


def apart_z(value, by):
    return along(value, "short", lambda i: i ^ by * RING)


def apart_x(value, by):
    return along(value, "long", lambda i: i ^ by * CORES)


def other_core(value):
    return along(value, "long", lambda i: i ^ 1)


def tied(value, *others):
    return lax.optimization_barrier((value, *others))[0]


def buckets_of_ring(parts):
    return parts[1], parts[2] + parts[3]


def per_device(query, key, value, level_weight):
    level_weight = jnp.transpose(level_weight, (1, 0, 2))
    core = place()[1]
    state, *quarters = states(key, value)
    quarters = [quarters[0]] + [apart_y(quarters[m], m) for m in (1, 2, 3)]
    query_h, key_h, value_t = by_head(tied(query, state), key, value)
    first = apart_y(state, 1)
    heads = query_h.shape[0]
    share = heads // RING

    quarters = tied(quarters, query_h)
    ring_y = sum(quarters[1:], quarters[0])

    def near_of(head, count, tie, mib):
        return near_part(query_h, key_h, value_t, level_weight, tie, head, count, mib)

    sums = [ring_y] + [apart_z(ring_y, m) for m in (1, 2, 3)]
    near = [near_of(0, EARLY_HEADS, ring_y, 12)]
    sums = tied(sums, near[0])
    ring_z = sum(sums[1:], sums[0])
    facing = other_core(ring_z)
    first = tied(first, ring_z)
    facing = tied(facing, first)
    near_buckets = jnp.stack(buckets_of_ring(sums))
    inner = [near_buckets, apart_y(near_buckets, 1), None, None]

    mine = lax.dynamic_slice_in_dim(ring_z, core, 1, 0)
    theirs = lax.dynamic_slice_in_dim(facing, core, 1, 0)
    chip = mine + theirs
    chip_first = apart_x(chip, 1)
    pair = state + tied(first, chip)
    second = apart_y(pair, 3)
    inner[3] = apart_y(tied(near_buckets, chip), 3)
    chip_first = tied(chip_first, pair)
    chip_second = apart_x(chip + chip_first, 3)
    chip_second = tied(chip_second, inner[1], inner[3])
    outer = jnp.stack([jnp.where(core == 0, mine, theirs), chip_first, chip_second])
    outer = [outer] + [apart_y(outer, m) for m in (1, 2, 3)]
    inner[2] = apart_y(inner[3], 1)
    near.append(near_of(EARLY_HEADS, heads - EARLY_HEADS, outer[0], 12))

    def owner(m):
        return lambda p: (p[0] ^ m) * share

    pieces = [(first[None], (0,), lambda p: 0), (second[None], (1,), lambda p: 0)]
    pieces += [(inner[m], (2, 3), owner(m)) for m in range(RING)]
    total = far_part(query_h, level_weight, near, (0, 1, 2, 3), pieces, False)
    outer = tied(outer, total)
    outer_facing = [other_core(piece) for piece in outer]
    pieces = [(outer[m], (4, 5, 6), lambda p, m=m: owner(m)(p) + p[1]) for m in range(RING)]
    pieces += [
        (outer_facing[m], (4, 5, 6), lambda p, m=m: owner(m)(p) + 1 - p[1]) for m in range(RING)
    ]
    return far_part(query_h, level_weight, [total], (4, 5, 6), pieces, True)


def solution(mesh):
    return jax.shard_map(
        per_device,
        mesh=mesh,
        in_specs=(
            P(("long", "short"), None, None),
            P(("long", "short"), None, None),
            P(("long", "short"), None, None),
            P(None, None, ("long", "short")),
        ),
        out_specs=P(("long", "short"), None, None),
        check_vma=False,
    )
```

```python
import functools

import jax
import jax.numpy as jnp
from jax import lax
from jax.experimental import pallas as pl
from jax.experimental.pallas import tpu as pltpu
from jax.sharding import PartitionSpec as P

EPSILON = 1e-06
MIB = 1024 * 1024
NT = (((1,), (1,)), ((), ()))
NN = (((1,), (0,)), ((), ()))
RING = 4
CORES = 2
TILE = 256
EARLY_HEADS = 4
ROWS = 512


def dot(lhs, rhs, dims):
    return lax.dot_general(lhs, rhs, dims, preferred_element_type=jnp.float32)


def params(mib):
    return pltpu.CompilerParams(vmem_limit_bytes=mib * MIB)


def cost(flops, mib):
    return pl.CostEstimate(flops=int(flops), bytes_accessed=int(mib * MIB), transcendentals=0)


def place():
    short_pos = lax.axis_index("short").astype(jnp.int32)
    long_pos = lax.axis_index("long").astype(jnp.int32)
    block = long_pos * lax.axis_size("short") + short_pos
    return short_pos & (RING - 1), long_pos & (CORES - 1), block


def state_kernel(key_ref, value_ref, state_ref, *quarter_refs):
    step = pl.program_id(0)

    @pl.when(step == 0)
    def _():
        state_ref[...] = jnp.zeros_like(state_ref)

    keys = jnp.swapaxes(key_ref[...], 0, 1)
    values = jnp.swapaxes(value_ref[...], 0, 1)
    heads = keys.shape[0]
    for head in range(heads):
        state_ref[head] += dot(values[head].T, keys[head], NN)

    @pl.when(step == pl.num_programs(0) - 1)
    def _():
        share = heads // RING
        for apart in range(RING):
            owner = place()[0] ^ apart
            quarter_refs[apart][...] = state_ref[pl.ds(owner * share, share)]


def states(key, value, rows=512):
    length, heads, width = key.shape
    share = heads // RING
    part = pl.BlockSpec((rows, heads, width), lambda i: (i, 0, 0))
    return pl.pallas_call(
        state_kernel,
        grid=(length // rows,),
        in_specs=[part, part],
        out_specs=[pl.BlockSpec((heads, width, width), lambda i: (0, 0, 0))]
        + [pl.BlockSpec((share, width, width), lambda i: (0, 0, 0))] * RING,
        out_shape=[jax.ShapeDtypeStruct((heads, width, width), jnp.float32)]
        + [jax.ShapeDtypeStruct((share, width, width), jnp.float32)] * RING,
        compiler_params=params(60),
        cost_estimate=cost(3e8, 5),
        name="states",
    )(key, value)


def layout_kernel(query_ref, key_ref, value_ref, query_out, key_out, value_out):
    query_out[...] = jnp.swapaxes(query_ref[...], 0, 1)
    key_out[...] = jnp.swapaxes(key_ref[...], 0, 1)
    values = jnp.swapaxes(value_ref[...], 0, 1)
    for head in range(values.shape[0]):
        value_out[head] = values[head].T


def by_head(query, key, value, rows=512):
    length, heads, width = query.shape
    part = pl.BlockSpec((rows, heads, width), lambda i: (i, 0, 0))
    rowwise = pl.BlockSpec((heads, rows, width), lambda i: (0, i, 0))
    return pl.pallas_call(
        layout_kernel,
        grid=(length // rows,),
        in_specs=[part] * 3,
        out_specs=[rowwise, rowwise, pl.BlockSpec((heads, width, rows), lambda i: (0, 0, i))],
        out_shape=[jax.ShapeDtypeStruct((heads, length, width), jnp.bfloat16)] * 2
        + [jax.ShapeDtypeStruct((heads, width, length), jnp.bfloat16)],
        compiler_params=params(24),
        cost_estimate=cost(1e6, 0.01),
        name="by_head",
    )(query, key, value)


def near_kernel(first, query_ref, key_ref, value_ref, weight_ref, tie_ref, near_ref):
    length = query_ref.shape[1]
    head = pl.program_id(0) + first
    groups = TILE // 8
    group_r = lax.broadcasted_iota(jnp.int32, (groups, TILE), 0)
    group_t = lax.broadcasted_iota(jnp.int32, (groups, TILE), 1) >> 3
    apart = group_r ^ group_t
    later = group_t > group_r
    inner_s = lax.broadcasted_iota(jnp.int32, (8, TILE), 0)
    inner_t = lax.broadcasted_iota(jnp.int32, (8, TILE), 1) & 7
    inner = inner_s ^ inner_t
    same = (
        lax.broadcasted_iota(jnp.int32, (groups, 8, TILE), 0)
        == lax.broadcasted_iota(jnp.int32, (groups, 8, TILE), 2) >> 3
    )
    for tile in range(length // TILE):
        cols = slice(tile * TILE, (tile + 1) * TILE)

        def gain(level):
            return weight_ref[level, pl.ds(head, 1), cols]

        query = query_ref[0, cols, :]
        parts = []
        for other in range(tile):
            scores = dot(key_ref[0, other * TILE : (other + 1) * TILE, :], query, NT)
            parts.append((scores * gain(8 + (tile ^ other).bit_length())).astype(jnp.bfloat16))
        outer = gain(4)
        for level in range(5, 9):
            outer = jnp.where(apart >= 1 << (level - 4), gain(level), outer)
        outer = jnp.where(later, outer, 0.0)
        small = gain(0)
        for level in range(1, 4):
            small = jnp.where(inner >= 1 << (level - 1), gain(level), small)
        small = jnp.where(inner_s <= inner_t, small, 0.0)
        mixing = jnp.where(same, small[None], outer[:, None, :]).reshape(TILE, TILE)
        scores = dot(key_ref[0, cols, :], query, NT)
        parts.append((scores * mixing).astype(jnp.bfloat16))
        weighted = jnp.concatenate(parts, 0)
        near_ref[0, :, cols] = dot(value_ref[0, :, : (tile + 1) * TILE], weighted, NN)


def near_part(query, key, value, level_weight, tie, first, count, mib):
    heads, length, width = query.shape
    levels = level_weight.shape[0]
    rows = pl.BlockSpec((1, length, width), lambda h: (h + first, 0, 0))
    flat = pl.BlockSpec((1, width, length), lambda h: (h + first, 0, 0))
    return pl.pallas_call(
        functools.partial(near_kernel, first),
        grid=(count,),
        in_specs=[
            rows,
            rows,
            flat,
            pl.BlockSpec((levels, heads, length), lambda h: (0, 0, 0)),
            pl.BlockSpec(memory_space=pl.ANY),
        ],
        out_specs=pl.BlockSpec((1, width, length), lambda h: (h, 0, 0)),
        out_shape=jax.ShapeDtypeStruct((count, width, length), jnp.float32),
        compiler_params=params(mib),
        cost_estimate=cost(1e6, 0.01),
        name="near",
    )(query, key, value, level_weight, tie)


def far_kernel(plan, last, local_bits, query_ref, weight_ref, *rest):
    count, bits, pieces = plan
    total_refs, rest = rest[:count], rest[count:]
    piece_refs, rest = rest[: len(pieces)], rest[len(pieces) :]
    if last:
        out_ref, split, result, sent = rest
    else:
        out_ref, split = rest
    heads, length, width = query_ref.shape
    for ref, (piece_bits, first_head) in zip(piece_refs, pieces):
        base = first_head(place())
        for at, bit in enumerate(piece_bits):
            for head in range(ref.shape[1]):
                bucket = ref[at, head]
                high = bucket.astype(jnp.bfloat16)
                low = (bucket - high.astype(jnp.float32)).astype(jnp.bfloat16)
                where = bits.index(bit) * width
                split[base + head, where : where + width, :width] = high
                split[base + head, where : where + width, width:] = low

    block = place()[2]
    held = [(ref, at) for ref in total_refs for at in range(ref.shape[0])]
    copies = []
    rows = ROWS // 2 if last else ROWS
    for start in range(0, length, rows):
        cols = slice(start, start + rows)
        done = []
        for head in range(heads):
            query = query_ref[head, cols, :]
            products = dot(split[head], jnp.concatenate([query, query], 1), NT)
            ref, at = held[head]
            total = ref[at, :, cols]
            for at, bit in enumerate(bits):
                gain = weight_ref[local_bits + 1 + bit, head : head + 1, cols]
                gain = jnp.where((block >> bit) & 1 == 1, gain, 0.0)
                total = total + products[at * width : (at + 1) * width, :] * gain
            if last:
                mean = jnp.sum(total * total, 0, keepdims=True) * (1.0 / width)
                done.append((total * lax.rsqrt(mean + EPSILON)).astype(jnp.bfloat16).T)
            else:
                out_ref[head, :, cols] = total
        if last:
            result[cols] = jnp.swapaxes(jnp.stack(done), 0, 1)
            copies.append(
                pltpu.make_async_copy(result.at[cols], out_ref.at[cols], sent.at[len(copies)])
            )
            copies[-1].start()
    for copy in copies:
        copy.wait()


def far_part(query, level_weight, totals, bits, pieces, last):
    heads, length, width = query.shape
    local_bits = length.bit_length() - 1
    plan = (len(totals), bits, [(piece_bits, first) for _, piece_bits, first in pieces])
    arrays = [array for array, _, _ in pieces]
    scratch = [pltpu.VMEM((heads, len(bits) * width, 2 * width), jnp.bfloat16)]
    if last:
        scratch.append(pltpu.VMEM((length, heads, width), jnp.bfloat16))
        scratch.append(pltpu.SemaphoreType.DMA((2 * length // ROWS,)))
    held = pl.BlockSpec(memory_space=pltpu.VMEM)
    return pl.pallas_call(
        functools.partial(far_kernel, plan, last, local_bits),
        in_specs=[held] * (2 + len(totals) + len(arrays)),
        out_specs=pl.BlockSpec(memory_space=pl.ANY) if last else held,
        out_shape=jax.ShapeDtypeStruct((length, heads, width), jnp.bfloat16)
        if last
        else jax.ShapeDtypeStruct((heads, width, length), jnp.float32),
        scratch_shapes=scratch,
        compiler_params=params(24),
        cost_estimate=cost(1e6, 0.01),
        name="finish" if last else "far",
    )(query, level_weight, *totals, *arrays)


def along(value, axis, hop):
    return lax.ppermute(value, axis, [(i, hop(i)) for i in range(lax.axis_size(axis))])


def apart_y(value, by):
    return along(value, "short", lambda i: i ^ by)


def apart_z(value, by):
    return along(value, "short", lambda i: i ^ by * RING)


def apart_x(value, by):
    return along(value, "long", lambda i: i ^ by * CORES)


def other_core(value):
    return along(value, "long", lambda i: i ^ 1)


def tied(value, *others):
    return lax.optimization_barrier((value, *others))[0]


def buckets_of_ring(parts):
    return parts[1], parts[2] + parts[3]


def per_device(query, key, value, level_weight):
    level_weight = jnp.transpose(level_weight, (1, 0, 2))
    core = place()[1]
    state, *quarters = states(key, value)
    quarters = [quarters[0]] + [apart_y(quarters[m], m) for m in (1, 2, 3)]
    query_h, key_h, value_t = by_head(tied(query, state), key, value)
    first = apart_y(state, 1)
    heads = query_h.shape[0]
    share = heads // RING

    quarters = tied(quarters, query_h)
    ring_y = sum(quarters[1:], quarters[0])

    def near_of(head, count, tie, mib):
        return near_part(query_h, key_h, value_t, level_weight, tie, head, count, mib)

    sums = [ring_y] + [apart_z(ring_y, m) for m in (1, 2, 3)]
    near = [near_of(0, EARLY_HEADS, ring_y, 12)]
    sums = tied(sums, near[0])
    ring_z = sum(sums[1:], sums[0])
    facing = other_core(ring_z)
    first = tied(first, ring_z)
    facing = tied(facing, first)
    near_buckets = jnp.stack(buckets_of_ring(sums))
    inner = [near_buckets, apart_y(near_buckets, 1), None, apart_y(near_buckets, 3)]

    mine = lax.dynamic_slice_in_dim(ring_z, core, 1, 0)
    theirs = lax.dynamic_slice_in_dim(facing, core, 1, 0)
    chip = mine + theirs
    chip_first = apart_x(chip, 1)
    pair = state + tied(first, chip)
    second = apart_y(pair, 3)
    chip_first = tied(chip_first, pair)
    chip_second = apart_x(chip + chip_first, 3)
    chip_second = tied(chip_second, inner[1], inner[3])
    outer = jnp.stack([jnp.where(core == 0, mine, theirs), chip_first, chip_second])
    outer = [outer] + [apart_y(outer, m) for m in (1, 2, 3)]
    inner[2] = apart_y(inner[3], 1)
    near.append(near_of(EARLY_HEADS, heads - EARLY_HEADS, outer[0], 12))

    def owner(m):
        return lambda p: (p[0] ^ m) * share

    pieces = [(first[None], (0,), lambda p: 0), (second[None], (1,), lambda p: 0)]
    pieces += [(inner[m], (2, 3), owner(m)) for m in range(RING)]
    total = far_part(query_h, level_weight, near, (0, 1, 2, 3), pieces, False)
    outer = tied(outer, total)
    outer_facing = [other_core(piece) for piece in outer]
    pieces = [(outer[m], (4, 5, 6), lambda p, m=m: owner(m)(p) + p[1]) for m in range(RING)]
    pieces += [
        (outer_facing[m], (4, 5, 6), lambda p, m=m: owner(m)(p) + 1 - p[1]) for m in range(RING)
    ]
    return far_part(query_h, level_weight, [total], (4, 5, 6), pieces, True)


def solution(mesh):
    return jax.shard_map(
        per_device,
        mesh=mesh,
        in_specs=(
            P(("long", "short"), None, None),
            P(("long", "short"), None, None),
            P(("long", "short"), None, None),
            P(None, None, ("long", "short")),
        ),
        out_specs=P(("long", "short"), None, None),
        check_vma=False,
    )
```

```python
import functools

import jax
import jax.numpy as jnp
from jax import lax
from jax.experimental import pallas as pl
from jax.experimental.pallas import tpu as pltpu
from jax.sharding import PartitionSpec as P

EPSILON = 1e-06
MIB = 1024 * 1024
NT = (((1,), (1,)), ((), ()))
NN = (((1,), (0,)), ((), ()))
RING = 4
CORES = 2
TILE = 256
EARLY_HEADS = 3
ROWS = 512


def dot(lhs, rhs, dims):
    return lax.dot_general(lhs, rhs, dims, preferred_element_type=jnp.float32)


def params(mib):
    return pltpu.CompilerParams(vmem_limit_bytes=mib * MIB)


def cost(flops, mib):
    return pl.CostEstimate(flops=int(flops), bytes_accessed=int(mib * MIB), transcendentals=0)


def place():
    short_pos = lax.axis_index("short").astype(jnp.int32)
    long_pos = lax.axis_index("long").astype(jnp.int32)
    block = long_pos * lax.axis_size("short") + short_pos
    return short_pos & (RING - 1), long_pos & (CORES - 1), block


def state_kernel(key_ref, value_ref, state_ref, *quarter_refs):
    step = pl.program_id(0)

    @pl.when(step == 0)
    def _():
        state_ref[...] = jnp.zeros_like(state_ref)

    keys = jnp.swapaxes(key_ref[...], 0, 1)
    values = jnp.swapaxes(value_ref[...], 0, 1)
    heads = keys.shape[0]
    for head in range(heads):
        state_ref[head] += dot(values[head].T, keys[head], NN)

    @pl.when(step == pl.num_programs(0) - 1)
    def _():
        share = heads // RING
        for apart in range(RING):
            owner = place()[0] ^ apart
            quarter_refs[apart][...] = state_ref[pl.ds(owner * share, share)]


def states(key, value, rows=512):
    length, heads, width = key.shape
    share = heads // RING
    part = pl.BlockSpec((rows, heads, width), lambda i: (i, 0, 0))
    return pl.pallas_call(
        state_kernel,
        grid=(length // rows,),
        in_specs=[part, part],
        out_specs=[pl.BlockSpec((heads, width, width), lambda i: (0, 0, 0))]
        + [pl.BlockSpec((share, width, width), lambda i: (0, 0, 0))] * RING,
        out_shape=[jax.ShapeDtypeStruct((heads, width, width), jnp.float32)]
        + [jax.ShapeDtypeStruct((share, width, width), jnp.float32)] * RING,
        compiler_params=params(60),
        cost_estimate=cost(3e8, 5),
        name="states",
    )(key, value)


def layout_kernel(query_ref, key_ref, value_ref, query_out, key_out, value_out):
    query_out[...] = jnp.swapaxes(query_ref[...], 0, 1)
    key_out[...] = jnp.swapaxes(key_ref[...], 0, 1)
    values = jnp.swapaxes(value_ref[...], 0, 1)
    for head in range(values.shape[0]):
        value_out[head] = values[head].T


def by_head(query, key, value, rows=512):
    length, heads, width = query.shape
    part = pl.BlockSpec((rows, heads, width), lambda i: (i, 0, 0))
    rowwise = pl.BlockSpec((heads, rows, width), lambda i: (0, i, 0))
    return pl.pallas_call(
        layout_kernel,
        grid=(length // rows,),
        in_specs=[part] * 3,
        out_specs=[rowwise, rowwise, pl.BlockSpec((heads, width, rows), lambda i: (0, 0, i))],
        out_shape=[jax.ShapeDtypeStruct((heads, length, width), jnp.bfloat16)] * 2
        + [jax.ShapeDtypeStruct((heads, width, length), jnp.bfloat16)],
        compiler_params=params(24),
        cost_estimate=cost(1e6, 0.01),
        name="by_head",
    )(query, key, value)


def near_kernel(first, query_ref, key_ref, value_ref, weight_ref, tie_ref, near_ref):
    length = query_ref.shape[1]
    head = pl.program_id(0) + first
    groups = TILE // 8
    group_r = lax.broadcasted_iota(jnp.int32, (groups, TILE), 0)
    group_t = lax.broadcasted_iota(jnp.int32, (groups, TILE), 1) >> 3
    apart = group_r ^ group_t
    later = group_t > group_r
    inner_s = lax.broadcasted_iota(jnp.int32, (8, TILE), 0)
    inner_t = lax.broadcasted_iota(jnp.int32, (8, TILE), 1) & 7
    inner = inner_s ^ inner_t
    same = (
        lax.broadcasted_iota(jnp.int32, (groups, 8, TILE), 0)
        == lax.broadcasted_iota(jnp.int32, (groups, 8, TILE), 2) >> 3
    )
    for tile in range(length // TILE):
        cols = slice(tile * TILE, (tile + 1) * TILE)

        def gain(level):
            return weight_ref[level, pl.ds(head, 1), cols]

        query = query_ref[0, cols, :]
        parts = []
        for other in range(tile):
            scores = dot(key_ref[0, other * TILE : (other + 1) * TILE, :], query, NT)
            parts.append((scores * gain(8 + (tile ^ other).bit_length())).astype(jnp.bfloat16))
        outer = gain(4)
        for level in range(5, 9):
            outer = jnp.where(apart >= 1 << (level - 4), gain(level), outer)
        outer = jnp.where(later, outer, 0.0)
        small = gain(0)
        for level in range(1, 4):
            small = jnp.where(inner >= 1 << (level - 1), gain(level), small)
        small = jnp.where(inner_s <= inner_t, small, 0.0)
        mixing = jnp.where(same, small[None], outer[:, None, :]).reshape(TILE, TILE)
        scores = dot(key_ref[0, cols, :], query, NT)
        parts.append((scores * mixing).astype(jnp.bfloat16))
        weighted = jnp.concatenate(parts, 0)
        near_ref[0, :, cols] = dot(value_ref[0, :, : (tile + 1) * TILE], weighted, NN)


def near_part(query, key, value, level_weight, tie, first, count, mib):
    heads, length, width = query.shape
    levels = level_weight.shape[0]
    rows = pl.BlockSpec((1, length, width), lambda h: (h + first, 0, 0))
    flat = pl.BlockSpec((1, width, length), lambda h: (h + first, 0, 0))
    return pl.pallas_call(
        functools.partial(near_kernel, first),
        grid=(count,),
        in_specs=[
            rows,
            rows,
            flat,
            pl.BlockSpec((levels, heads, length), lambda h: (0, 0, 0)),
            pl.BlockSpec(memory_space=pl.ANY),
        ],
        out_specs=pl.BlockSpec((1, width, length), lambda h: (h, 0, 0)),
        out_shape=jax.ShapeDtypeStruct((count, width, length), jnp.float32),
        compiler_params=params(mib),
        cost_estimate=cost(1e6, 0.01),
        name="near",
    )(query, key, value, level_weight, tie)


def far_kernel(plan, last, local_bits, query_ref, weight_ref, *rest):
    count, bits, pieces = plan
    total_refs, rest = rest[:count], rest[count:]
    piece_refs, rest = rest[: len(pieces)], rest[len(pieces) :]
    if last:
        out_ref, split, result, sent = rest
    else:
        out_ref, split = rest
    heads, length, width = query_ref.shape
    for ref, (piece_bits, first_head) in zip(piece_refs, pieces):
        base = first_head(place())
        for at, bit in enumerate(piece_bits):
            for head in range(ref.shape[1]):
                bucket = ref[at, head]
                high = bucket.astype(jnp.bfloat16)
                low = (bucket - high.astype(jnp.float32)).astype(jnp.bfloat16)
                where = bits.index(bit) * width
                split[base + head, where : where + width, :width] = high
                split[base + head, where : where + width, width:] = low

    block = place()[2]
    held = [(ref, at) for ref in total_refs for at in range(ref.shape[0])]
    copies = []
    rows = ROWS // 2 if last else ROWS
    for start in range(0, length, rows):
        cols = slice(start, start + rows)
        done = []
        for head in range(heads):
            query = query_ref[head, cols, :]
            products = dot(split[head], jnp.concatenate([query, query], 1), NT)
            ref, at = held[head]
            total = ref[at, :, cols]
            for at, bit in enumerate(bits):
                gain = weight_ref[local_bits + 1 + bit, head : head + 1, cols]
                gain = jnp.where((block >> bit) & 1 == 1, gain, 0.0)
                total = total + products[at * width : (at + 1) * width, :] * gain
            if last:
                mean = jnp.sum(total * total, 0, keepdims=True) * (1.0 / width)
                done.append((total * lax.rsqrt(mean + EPSILON)).astype(jnp.bfloat16).T)
            else:
                out_ref[head, :, cols] = total
        if last:
            result[cols] = jnp.swapaxes(jnp.stack(done), 0, 1)
            copies.append(
                pltpu.make_async_copy(result.at[cols], out_ref.at[cols], sent.at[len(copies)])
            )
            copies[-1].start()
    for copy in copies:
        copy.wait()


def far_part(query, level_weight, totals, bits, pieces, last):
    heads, length, width = query.shape
    local_bits = length.bit_length() - 1
    plan = (len(totals), bits, [(piece_bits, first) for _, piece_bits, first in pieces])
    arrays = [array for array, _, _ in pieces]
    scratch = [pltpu.VMEM((heads, len(bits) * width, 2 * width), jnp.bfloat16)]
    if last:
        scratch.append(pltpu.VMEM((length, heads, width), jnp.bfloat16))
        scratch.append(pltpu.SemaphoreType.DMA((2 * length // ROWS,)))
    held = pl.BlockSpec(memory_space=pltpu.VMEM)
    return pl.pallas_call(
        functools.partial(far_kernel, plan, last, local_bits),
        in_specs=[held] * (2 + len(totals) + len(arrays)),
        out_specs=pl.BlockSpec(memory_space=pl.ANY) if last else held,
        out_shape=jax.ShapeDtypeStruct((length, heads, width), jnp.bfloat16)
        if last
        else jax.ShapeDtypeStruct((heads, width, length), jnp.float32),
        scratch_shapes=scratch,
        compiler_params=params(24),
        cost_estimate=cost(1e6, 0.01),
        name="finish" if last else "far",
    )(query, level_weight, *totals, *arrays)


def along(value, axis, hop):
    return lax.ppermute(value, axis, [(i, hop(i)) for i in range(lax.axis_size(axis))])


def apart_y(value, by):
    return along(value, "short", lambda i: i ^ by)


def apart_z(value, by):
    return along(value, "short", lambda i: i ^ by * RING)


def apart_x(value, by):
    return along(value, "long", lambda i: i ^ by * CORES)


def other_core(value):
    return along(value, "long", lambda i: i ^ 1)


def tied(value, *others):
    return lax.optimization_barrier((value, *others))[0]


def buckets_of_ring(parts):
    return parts[1], parts[2] + parts[3]


def per_device(query, key, value, level_weight):
    level_weight = jnp.transpose(level_weight, (1, 0, 2))
    core = place()[1]
    state, *quarters = states(key, value)
    quarters = [quarters[0]] + [apart_y(quarters[m], m) for m in (1, 2, 3)]
    query_h, key_h, value_t = by_head(tied(query, state), key, value)
    first = apart_y(state, 1)
    heads = query_h.shape[0]
    share = heads // RING

    quarters = tied(quarters, query_h)
    ring_y = sum(quarters[1:], quarters[0])

    def near_of(head, count, tie, mib):
        return near_part(query_h, key_h, value_t, level_weight, tie, head, count, mib)

    sums = [ring_y] + [apart_z(ring_y, m) for m in (1, 2, 3)]
    near = [near_of(0, EARLY_HEADS, ring_y, 12)]
    sums = tied(sums, near[0])
    ring_z = sum(sums[1:], sums[0])
    facing = other_core(ring_z)
    first = tied(first, ring_z)
    facing = tied(facing, first)
    near_buckets = jnp.stack(buckets_of_ring(sums))
    inner = [near_buckets, apart_y(near_buckets, 1), None, apart_y(near_buckets, 3)]

    mine = lax.dynamic_slice_in_dim(ring_z, core, 1, 0)
    theirs = lax.dynamic_slice_in_dim(facing, core, 1, 0)
    chip = mine + theirs
    chip_first = apart_x(chip, 1)
    pair = state + tied(first, chip)
    second = apart_y(pair, 3)
    chip_first = tied(chip_first, pair)
    chip_second = apart_x(chip + chip_first, 3)
    chip_second = tied(chip_second, inner[1], inner[3])
    outer = jnp.stack([jnp.where(core == 0, mine, theirs), chip_first, chip_second])
    outer = [outer] + [apart_y(outer, m) for m in (1, 2, 3)]
    inner[2] = apart_y(inner[3], 1)
    near.append(near_of(EARLY_HEADS, heads - EARLY_HEADS, outer[0], 12))

    def owner(m):
        return lambda p: (p[0] ^ m) * share

    pieces = [(first[None], (0,), lambda p: 0), (second[None], (1,), lambda p: 0)]
    pieces += [(inner[m], (2, 3), owner(m)) for m in range(RING)]
    total = far_part(query_h, level_weight, near, (0, 1, 2, 3), pieces, False)
    outer = tied(outer, total)
    outer_facing = [other_core(piece) for piece in outer]
    pieces = [(outer[m], (4, 5, 6), lambda p, m=m: owner(m)(p) + p[1]) for m in range(RING)]
    pieces += [
        (outer_facing[m], (4, 5, 6), lambda p, m=m: owner(m)(p) + 1 - p[1]) for m in range(RING)
    ]
    return far_part(query_h, level_weight, [total], (4, 5, 6), pieces, True)


def solution(mesh):
    return jax.shard_map(
        per_device,
        mesh=mesh,
        in_specs=(
            P(("long", "short"), None, None),
            P(("long", "short"), None, None),
            P(("long", "short"), None, None),
            P(None, None, ("long", "short")),
        ),
        out_specs=P(("long", "short"), None, None),
        check_vma=False,
    )
```
